32 devices in a mesh: tiles: 4 (over z), rows: 8 (over y, x, core).
Axes of the slice: x: 2, y: 2, z: 4, core: 2. Of those that a mesh axis runs over, the one named last changes fastest.
Arguments:
- tile_values: bfloat16 [32, 8, 1024, 1024], P(('tiles', 'rows')), may hold values from -6 to 6
- tile_coords: int32 [32, 8, 4], P(('tiles', 'rows')), may hold values from 0 to 95, as said below
- tile_count: int32 [32], P(('tiles', 'rows')), may hold values from 4 to 8, as said below
- factors: float32 [4, 3072, 256], P(None, 'rows'), may hold values from -3 to 3
Outputs:
- updated: float32 [4, 3072, 256], P(None, 'rows')
The draws below stay inside these ranges and needn't reach their ends.
Inputs may be any that keep to these rules, and one draw needn't show every extreme that they name: `tile_coords`: over the live slots of one device, the four modes together name blocks of one row owner (block index // 12) at most 4 times; on every device some owner is named exactly 4 times. The same block may appear in several tiles. Slot 0 is always live. Slots from tile_count[d] on are ignored; some device has all slots live.
All inputs are finite; a program needn't handle non-finite values.
Results may differ from the reference program's by a relative error of at most 0.0033.
Values may be sent and summed in bfloat16 or wider, within the bound.
A program may use at most 128 MiB of HBM per device.

```python
import jax
import jax.numpy as jnp
from jax import lax

TILE = 32
RANK = 256
SLOTS = 8
CAP = 4
BLK_DEV = 12
NB = 3072
N_ROWS = 8
DEVICES = 32


def draw_tile_coords(key, part):
    key = jax.random.fold_in(key, 11)

    def one_device(device_key):
        key_owner, key_order, key_local = jax.random.split(device_key, 3)
        owners = jnp.repeat(jnp.arange(N_ROWS, dtype=jnp.int32), CAP)
        chosen = jax.random.randint(key_owner, (), 0, N_ROWS, dtype=jnp.int32)
        scores = jax.random.permutation(key_order, N_ROWS * CAP).astype(jnp.int32)
        scores = jnp.where(owners == chosen, scores - 2 * N_ROWS * CAP, scores)
        ordering = jnp.argsort(scores, stable=True)
        picked = owners[ordering][:SLOTS * 4].reshape(SLOTS, 4)
        local_part = jax.random.randint(key_local, (SLOTS, 4), 0, BLK_DEV, dtype=jnp.int32)
        return (picked * BLK_DEV + local_part).astype(jnp.int32)
    return jax.vmap(one_device)(jax.random.split(key, DEVICES))


def draw_tile_count(key, part):
    key = jax.random.fold_in(key, 23)
    key_count, key_full = jax.random.split(key)
    counts = jax.random.randint(key_count, (DEVICES,), 4, SLOTS + 1, dtype=jnp.int32)
    fullest = jax.random.randint(key_full, (), 0, DEVICES, dtype=jnp.int32)
    return counts.at[fullest].set(SLOTS).astype(jnp.int32)


def levels(stream_key, extent, cuts, smallest, high):
    gain = 1.0
    for axis_at, blocks in cuts:
        steps = jax.random.uniform(jax.random.fold_in(jax.random.fold_in(stream_key, 6), axis_at), (blocks,), jnp.float32, smallest / len(cuts), high / len(cuts))
        gain = gain * jnp.repeat(jnp.exp(steps), extent[axis_at] // blocks).reshape((-1,) + (1,) * (len(extent) - 1 - axis_at))
    return gain


def gaussian(stream_key, extent, spread, bound, shards=(), kind=jnp.bfloat16):
    gain = levels(stream_key, extent, shards, -0.22, 0.18) if shards else 1.0
    values = jax.random.normal(stream_key, extent, jnp.float32) * spread * gain
    return jnp.minimum(jnp.maximum(values, -bound), bound).astype(kind)


def setup_inputs(seed: int = 0) -> dict:
    splits = jax.random.split(jax.random.key(seed), 5)
    tile_values = gaussian(splits[0], (DEVICES, SLOTS, TILE * TILE, TILE * TILE), 1.0, 6.0, ((0, 32),))
    tile_coords = draw_tile_coords(jax.random.fold_in(splits[4], 71), 0)
    tile_count = draw_tile_count(jax.random.fold_in(splits[4], 71), 0)
    factors = gaussian(splits[3], (4, NB, RANK), 0.5, 3.0, ((1, 8),), jnp.float32)
    return dict(tile_values=tile_values, tile_coords=tile_coords, tile_count=tile_count, factors=factors)


step_size = 0.02


def rounded(array):
    return lax.optimization_barrier(array.astype(jnp.bfloat16)).astype(jnp.float32)


def tile_gradient(tile_block, blocks):
    mode_one, mode_two, mode_three, mode_four = blocks[0], blocks[1], blocks[2], blocks[3]
    tile_edge = mode_one.shape[0]
    pair_ab = rounded((mode_one[:, None, :] * mode_two[None, :, :]).reshape(tile_edge * tile_edge, RANK))
    pair_cd = rounded((mode_three[:, None, :] * mode_four[None, :, :]).reshape(tile_edge * tile_edge, RANK))
    model_values = jnp.dot(pair_ab, pair_cd.T, precision=lax.Precision.HIGHEST)
    misfit = rounded(jnp.clip(model_values - tile_block, -1.0, 1.0))
    left_terms = jnp.dot(misfit, pair_cd, precision=lax.Precision.HIGHEST).reshape(tile_edge, tile_edge, RANK)
    right_terms = jnp.dot(misfit.T, pair_ab, precision=lax.Precision.HIGHEST).reshape(tile_edge, tile_edge, RANK)
    grad_one = jnp.sum(left_terms * mode_two[None, :, :], axis=1)
    grad_two = jnp.sum(left_terms * mode_one[:, None, :], axis=0)
    grad_three = jnp.sum(right_terms * mode_four[None, :, :], axis=1)
    grad_four = jnp.sum(right_terms * mode_three[:, None, :], axis=0)
    return jnp.stack([grad_one, grad_two, grad_three, grad_four])


def reference(tile_values, tile_coords, tile_count, factors):
    narrow = rounded(factors)
    tile_rows = tile_values.reshape(DEVICES * SLOTS, TILE * TILE, TILE * TILE)
    coord_rows = tile_coords.reshape(DEVICES * SLOTS, 4)
    alive = (jnp.arange(SLOTS)[None, :] < tile_count[:, None]).reshape(DEVICES * SLOTS)
    zero_index = jnp.zeros((), jnp.int32)

    def visit(running, scan_item):
        tile_block, coord_row, alive_flag = scan_item
        starts = [(coord_row[mode] * TILE).astype(jnp.int32) for mode in range(4)]
        blocks = jnp.stack([lax.dynamic_slice_in_dim(narrow[mode], starts[mode], TILE, 0) for mode in range(4)])

        def compute():
            return tile_gradient(tile_block.astype(jnp.float32), blocks)

        def skipped():
            return jnp.zeros((4, TILE, RANK), jnp.float32)

        gradient = lax.cond(alive_flag, compute, skipped)
        for mode in range(4):
            anchor = (zero_index + mode, starts[mode], zero_index)
            current = lax.dynamic_slice(running, anchor, (1, TILE, RANK))
            running = lax.dynamic_update_slice(running, current + gradient[mode][None], anchor)
        return running, None

    running, unused = lax.scan(visit, jnp.zeros(factors.shape, jnp.float32), (tile_rows, coord_rows, alive))
    return factors - step_size * running
```

```python
import functools

import jax
import jax.numpy as jnp
from jax import lax
from jax.experimental import pallas as pl
from jax.experimental.pallas import tpu as pltpu
from jax.sharding import PartitionSpec as P

TILE = 32
CAP = 4
LANES = 128
MESH = pl.DeviceIdType.MESH

step_size = 0.02


def position(peers, rows):
    return lax.axis_index("tiles") * rows + lax.axis_index("rows")


def place(index, rows):
    return {"tiles": index // rows, "rows": lax.rem(index, rows)}


def enter(me, peers, rows):
    barrier = pltpu.get_barrier_semaphore()

    @pl.loop(1, peers)
    def _(k):
        other = lax.rem(me + k, peers)
        pl.semaphore_signal(barrier, inc=1, device_id=place(other, rows), device_id_type=MESH)

    pl.semaphore_wait(barrier, peers - 1)


def fetch_kernel(tiles, rows, want_ref, factors_ref, names_ref, blocks_ref, packed, scalars, name_send, name_recv, block_send, block_recv, local_sem):
    peers = tiles * rows
    my_tile, my_row = lax.axis_index("tiles"), lax.axis_index("rows")
    me = my_tile * rows + my_row
    enter(me, peers, rows)
    names_ref[me] = want_ref[...]

    def name_copy(other, slot, sem):
        return pltpu.make_async_remote_copy(
            src_ref=want_ref, dst_ref=names_ref.at[slot], send_sem=name_send.at[sem], recv_sem=name_recv.at[slot],
            device_id=place(other, rows), device_id_type=MESH)

    @pl.loop(1, rows)
    def _(k):
        other = my_tile * rows + lax.rem(my_row + k, rows)
        name_copy(other, me, other).start()

    @pl.loop(1, tiles)
    def _(j):
        @pl.loop(0, rows)
        def _(k):
            other = lax.rem(my_tile + j, tiles) * rows + lax.rem(my_row + k, rows)
            name_copy(other, me, other).start()

    @pl.loop(1, rows)
    def _(k):
        other = my_tile * rows + lax.rem(my_row + k, rows)
        name_copy(other, other, other).wait_recv()

    bring = pltpu.make_async_copy(names_ref.at[pl.ds(my_tile * rows, rows)], scalars, local_sem)
    bring.start()
    bring.wait()

    def block_copy(peer, slot):
        return pltpu.make_async_remote_copy(
            src_ref=packed.at[peer], dst_ref=blocks_ref.at[slot], send_sem=block_send.at[peer], recv_sem=block_recv.at[slot],
            device_id=place(my_tile * rows + peer, rows), device_id_type=MESH)

    def read(peer, rank):
        return factors_ref[jnp.maximum(scalars[peer, 0, my_row * CAP + rank], 0)].astype(jnp.bfloat16)

    @pl.loop(1, rows)
    def _(k):
        peer = lax.rem(my_row + k, rows)
        for rank in range(CAP):
            packed[peer, pl.ds(rank * TILE, TILE), :] = read(peer, rank)
        block_copy(peer, my_row).start()

    for rank in range(CAP):
        blocks_ref[my_row, pl.ds(rank * TILE, TILE), :] = read(my_row, rank)

    @pl.loop(1, rows)
    def _(k):
        peer = lax.rem(my_row + k, rows)
        block_copy(peer, peer).wait_recv()
        block_copy(peer, my_row).wait_send()
        other = my_tile * rows + peer
        name_copy(other, me, other).wait_send()

    @pl.loop(1, tiles)
    def _(j):
        @pl.loop(0, rows)
        def _(k):
            other = lax.rem(my_tile + j, tiles) * rows + lax.rem(my_row + k, rows)
            name_copy(other, other, other).wait_recv()
            name_copy(other, me, other).wait_send()


def fetch(want, factors, tiles, rows):
    rank = factors.shape[2]
    peers = tiles * rows
    return pl.pallas_call(
        functools.partial(fetch_kernel, tiles, rows),
        out_shape=(
            jax.ShapeDtypeStruct((peers, 1, LANES), jnp.int32),
            jax.ShapeDtypeStruct((rows, CAP * TILE, rank), jnp.bfloat16),
        ),
        in_specs=[pl.BlockSpec(memory_space=pltpu.VMEM)] * 2,
        out_specs=[pl.BlockSpec(memory_space=pltpu.VMEM)] * 2,
        scratch_shapes=[
            pltpu.VMEM((rows, CAP * TILE, rank), jnp.bfloat16),
            pltpu.SMEM((rows, 1, LANES), jnp.int32),
            pltpu.SemaphoreType.DMA((peers,)),
            pltpu.SemaphoreType.DMA((peers,)),
            pltpu.SemaphoreType.DMA((rows,)),
            pltpu.SemaphoreType.DMA((rows,)),
            pltpu.SemaphoreType.DMA,
        ],
        compiler_params=pltpu.CompilerParams(collective_id=0, has_side_effects=True, vmem_limit_bytes=32 << 20),
        name="fetch_blocks",
    )(want, factors)


def tile_kernel(pos_ref, count_ref, tile_ref, blocks_ref, grads_ref, pair_ab, pair_cd, misfit):
    slot = pl.program_id(0)
    edge = TILE
    chunk = 256
    group = chunk // edge
    rank = blocks_ref.shape[2]

    @pl.when(slot < count_ref[0])
    def _():
        one, two, three, four = (blocks_ref[pos_ref[slot * 4 + mode]].astype(jnp.float32) for mode in range(4))
        for part in range(edge // group):
            lines = slice(part * group, (part + 1) * group)
            place_at = pl.ds(part * chunk, chunk)
            pair_ab[place_at, :] = (one[lines][:, None, :] * two[None, :, :]).reshape(chunk, rank).astype(jnp.bfloat16)
            pair_cd[place_at, :] = (three[lines][:, None, :] * four[None, :, :]).reshape(chunk, rank).astype(jnp.bfloat16)
        second = jnp.zeros((edge, rank), jnp.float32)
        for part in range(edge // group):
            lines = slice(part * group, (part + 1) * group)
            place_at = pl.ds(part * chunk, chunk)
            model = lax.dot_general(pair_ab[place_at, :], pair_cd[...], (((1,), (1,)), ((), ())), preferred_element_type=jnp.float32)
            off = jnp.clip(model - tile_ref[0, place_at, :].astype(jnp.float32), -1.0, 1.0).astype(jnp.bfloat16)
            misfit[place_at, :] = off
            left = jnp.dot(off, pair_cd[...], preferred_element_type=jnp.float32).reshape(group, edge, rank)
            grads_ref[0, 0, lines, :] = jnp.sum(left * two[None, :, :], axis=1)
            second = second + jnp.sum(left * one[lines][:, None, :], axis=0)
        grads_ref[0, 1] = second
        fourth = jnp.zeros((edge, rank), jnp.float32)
        for part in range(edge // group):
            lines = slice(part * group, (part + 1) * group)
            place_at = pl.ds(part * chunk, chunk)
            right = lax.dot_general(misfit[:, place_at], pair_ab[...], (((0,), (0,)), ((), ())), preferred_element_type=jnp.float32).reshape(group, edge, rank)
            grads_ref[0, 2, lines, :] = jnp.sum(right * four[None, :, :], axis=1)
            fourth = fourth + jnp.sum(right * three[lines][:, None, :], axis=0)
        grads_ref[0, 3] = fourth


def tile_gradients(pos, count, tile_stack, blocks):
    slots, height, width = tile_stack.shape
    rank = blocks.shape[2]
    return pl.pallas_call(
        tile_kernel,
        out_shape=jax.ShapeDtypeStruct((slots, 4, TILE, rank), jnp.float32),
        grid_spec=pltpu.PrefetchScalarGridSpec(
            num_scalar_prefetch=2,
            grid=(slots,),
            in_specs=[
                pl.BlockSpec((1, height, width), lambda s, pos, count: (jnp.minimum(s, count[0] - 1), 0, 0)),
                pl.BlockSpec(memory_space=pltpu.VMEM),
            ],
            out_specs=pl.BlockSpec((1, 4, TILE, rank), lambda s, pos, count: (s, 0, 0, 0)),
            scratch_shapes=[
                pltpu.VMEM((height, rank), jnp.bfloat16),
                pltpu.VMEM((width, rank), jnp.bfloat16),
                pltpu.VMEM((height, width), jnp.bfloat16),
            ],
        ),
        compiler_params=pltpu.CompilerParams(vmem_limit_bytes=40 << 20),
        cost_estimate=pl.CostEstimate(flops=6 * slots * height * width * rank, bytes_accessed=2 * slots * height * width, transcendentals=0),
        name="tile_gradients",
    )(pos, count, tile_stack, blocks)


def reduce_kernel(tiles, rows, inverse_ref, names_ref, grads_ref, factors_ref, out_ref, packed, landed, target, gathered, send_sem, recv_sem, all_send, all_recv):
    peers = tiles * rows
    my_tile, my_row = lax.axis_index("tiles"), lax.axis_index("rows")
    me = my_tile * rows + my_row
    share = TILE // tiles
    span = CAP * share
    local = factors_ref.shape[0]
    rank = grads_ref.shape[2]
    enter(me, peers, rows)

    def message(other, slot):
        return pltpu.make_async_remote_copy(
            src_ref=packed.at[other], dst_ref=landed.at[slot], send_sem=send_sem.at[other], recv_sem=recv_sem.at[slot],
            device_id=place(other, rows), device_id_type=MESH)

    @pl.loop(0, rows)
    def _(k):
        owner = lax.rem(my_row + k, rows)
        found = []
        for spot in range(CAP):
            index = inverse_ref[0, owner * CAP + spot]
            block = grads_ref[jnp.maximum(index, 0)]
            found.append(jnp.where(index >= 0, block, 0.0))
        for tile in range(tiles):
            lines = slice(tile * share, (tile + 1) * share)
            packed[tile * rows + owner] = jnp.concatenate([block[lines] for block in found], axis=0).astype(jnp.bfloat16)

        @pl.when(k > 0)
        def _():
            message(my_tile * rows + owner, me).start()

        @pl.loop(1, tiles)
        def _(j):
            message(lax.rem(my_tile + j, tiles) * rows + owner, me).start()

    landed[me] = packed[me]
    inside = lax.broadcasted_iota(jnp.int32, (span, LANES), 0)

    @pl.loop(0, peers)
    def _(source):
        base = jnp.zeros((span, LANES), jnp.int32)
        for spot in range(CAP):
            name = names_ref[source, my_row * CAP + spot]
            line = jnp.where(name >= 0, name * share - spot * share, -(1 << 20))
            base = jnp.where(inside // share == spot, line, base)
        target[pl.ds(source * span, span), :] = base + inside

    @pl.loop(1, peers)
    def _(k):
        other = lax.rem(me + k, peers)
        message(other, other).wait_recv()

    total = local // TILE * share
    marks = [
        jnp.where(target[...] == lax.broadcasted_iota(jnp.int32, (peers * span, LANES), 1) + at, 1.0, 0.0).astype(jnp.bfloat16)
        for at in range(0, total, LANES)
    ]
    everything = landed[...].reshape(peers * span, rank)
    for at, mark in zip(range(0, total, LANES), marks):
        size = min(LANES, total - at)
        summed = lax.dot_general(mark, everything, (((0,), (0,)), ((), ())), preferred_element_type=jnp.float32)
        gathered[my_tile, pl.ds(at, size), :] = summed[:size].astype(jnp.bfloat16)

    def spread(other, slot):
        return pltpu.make_async_remote_copy(
            src_ref=gathered.at[my_tile], dst_ref=gathered.at[slot], send_sem=all_send.at[other], recv_sem=all_recv.at[slot],
            device_id=place(other * rows + my_row, rows), device_id_type=MESH)

    @pl.loop(1, tiles)
    def _(j):
        spread(lax.rem(my_tile + j, tiles), my_tile).start()

    per = 16 // share

    if share % 8 == 0:
        def update(tile):
            for at in range(0, total, 16):
                values = gathered[tile, pl.ds(at, 16), :].astype(jnp.float32)
                for piece in range(per):
                    line = pl.multiple_of((at // share + piece) * TILE + tile * share, share)
                    spot = pl.ds(line, share)
                    out_ref[spot, :] = factors_ref[spot, :] - step_size * values[piece * share:(piece + 1) * share]

        update(my_tile)

        @pl.loop(1, tiles)
        def _(j):
            other = lax.rem(my_tile + j, tiles)
            spread(other, other).wait_recv()
            update(other)
    else:
        @pl.loop(1, tiles)
        def _(j):
            other = lax.rem(my_tile + j, tiles)
            spread(other, other).wait_recv()

        for at in range(0, total, 16):
            values = [gathered[tile, pl.ds(at, 16), :].astype(jnp.float32) for tile in range(tiles)]
            for piece in range(per):
                spot = pl.ds((at // share + piece) * TILE, TILE)
                block = jnp.concatenate([value[piece * share:(piece + 1) * share] for value in values], axis=0)
                out_ref[spot, :] = factors_ref[spot, :] - step_size * block

    @pl.loop(1, tiles)
    def _(j):
        spread(lax.rem(my_tile + j, tiles), my_tile).wait_send()

    @pl.loop(1, peers)
    def _(k):
        message(lax.rem(me + k, peers), me).wait_send()


def reduce_update(inverse, names, grads, factors, tiles, rows):
    peers = tiles * rows
    local, rank = factors.shape
    share = TILE // tiles
    span = CAP * share
    total = local // TILE * share
    return pl.pallas_call(
        functools.partial(reduce_kernel, tiles, rows),
        out_shape=jax.ShapeDtypeStruct((local, rank), jnp.float32),
        in_specs=[pl.BlockSpec(memory_space=pltpu.SMEM)] * 2 + [pl.BlockSpec(memory_space=pltpu.VMEM)] * 2,
        out_specs=pl.BlockSpec(memory_space=pltpu.VMEM),
        scratch_shapes=[
            pltpu.VMEM((peers, span, rank), jnp.bfloat16),
            pltpu.VMEM((peers, span, rank), jnp.bfloat16),
            pltpu.VMEM((peers * span, LANES), jnp.int32),
            pltpu.VMEM((tiles, total, rank), jnp.bfloat16),
            pltpu.SemaphoreType.DMA((peers,)),
            pltpu.SemaphoreType.DMA((peers,)),
            pltpu.SemaphoreType.DMA((tiles,)),
            pltpu.SemaphoreType.DMA((tiles,)),
        ],
        compiler_params=pltpu.CompilerParams(collective_id=1, has_side_effects=True, vmem_limit_bytes=40 << 20),
        name="reduce_update",
    )(inverse, names, grads, factors)


def tables(coords, live_count, local_blocks):
    slots = coords.shape[0]
    names = slots * 4
    flat = coords.reshape(names)
    owner = flat // local_blocks
    order = jnp.arange(names)
    live = order // 4 < live_count
    earlier = (owner[None, :] == owner[:, None]) & live[None, :] & (order[None, :] < order[:, None])
    spot = owner * CAP + jnp.sum(earlier.astype(jnp.int32), axis=1)
    spot = jnp.where(live, spot, -1)
    hit = spot[None, :] == jnp.arange(LANES)[:, None]
    block = (order % 4) * local_blocks + flat - owner * local_blocks
    want = jnp.max(jnp.where(hit, block[None, :], -1), axis=1)
    inverse = jnp.max(jnp.where(hit, order[None, :], -1), axis=1)
    return jnp.maximum(spot, 0), want.reshape(1, LANES), inverse.reshape(1, LANES)


def on_device(tile_values, tile_coords, tile_count, factors):
    tiles, rows = lax.axis_size("tiles"), lax.axis_size("rows")
    modes, local_rows, rank = factors.shape
    spot, want, inverse = tables(tile_coords[0], tile_count[0], local_rows // TILE)
    flat = factors.reshape(modes * local_rows, rank)
    names, blocks = fetch(want, flat.reshape(-1, TILE, rank), tiles, rows)
    grads = tile_gradients(spot, tile_count, tile_values[0], blocks.reshape(rows * CAP, TILE, rank))
    slots = tile_values.shape[1]
    updated = reduce_update(inverse, names.reshape(tiles * rows, LANES), grads.reshape(slots * 4, TILE, rank), flat, tiles, rows)
    return updated.reshape(factors.shape)


def solution(mesh):
    return jax.shard_map(
        on_device,
        mesh=mesh,
        in_specs=(
            P(("tiles", "rows"), None, None, None),
            P(("tiles", "rows"), None, None),
            P(("tiles", "rows")),
            P(None, "rows", None),
        ),
        out_specs=P(None, "rows", None),
        check_vma=False,
    )
```

```python
import functools

import jax
import jax.numpy as jnp
from jax import lax
from jax.experimental import pallas as pl
from jax.experimental.pallas import tpu as pltpu
from jax.sharding import PartitionSpec as P

TILE = 32
CAP = 4
LANES = 128
MESH = pl.DeviceIdType.MESH

step_size = 0.02


def place(index, rows):
    return {"tiles": index // rows, "rows": lax.rem(index, rows)}


def step_kernel(
    tiles, rows, spot_ref, inverse_ref, want_ref, tile_hbm, factors_hbm, out_hbm,
    factors, stack, names, name_scalars, row_scalars, ask_packed, blocks, ab_even, ab_odd, cd_even, cd_odd, misfit_even, misfit_odd,
    grads, packed, landed, target, gathered,
    name_send, name_recv, block_send, block_recv, send_sem, recv_sem, up_send, down_send, all_recv, tile_sem, out_sem, local_sem,
):
    peers = tiles * rows
    my_tile, my_row = lax.axis_index("tiles"), lax.axis_index("rows")
    me = my_tile * rows + my_row
    slots = stack.shape[0]
    rank = factors.shape[2]
    row_place = lambda peer: my_tile * rows + peer
    far_place = lambda j, k: lax.rem(my_tile + j, tiles) * rows + lax.rem(my_row + k, rows)

    bring_factors = pltpu.make_async_copy(factors_hbm, factors, local_sem)
    bring_factors.start()
    barrier = pltpu.get_barrier_semaphore()
    for j in range(tiles):
        @pl.loop(0 if j else 1, rows, unroll=True)
        def _(k):
            pl.semaphore_signal(barrier, inc=1, device_id=place(far_place(j, k), rows), device_id_type=MESH)

    def tile_copy(slot):
        return pltpu.make_async_copy(tile_hbm.at[slot], stack.at[slot], tile_sem.at[slot])

    @pl.loop(0, slots)
    def _(slot):
        tile_copy(slot).start()

    names[me] = want_ref[...]
    bring_factors.wait()
    pl.semaphore_wait(barrier, peers - 1)

    def name_copy(other, slot):
        return pltpu.make_async_remote_copy(
            src_ref=want_ref, dst_ref=names.at[slot], send_sem=name_send.at[other], recv_sem=name_recv.at[slot],
            device_id=place(other, rows), device_id_type=MESH)

    @pl.loop(1, rows, unroll=True)
    def _(k):
        name_copy(row_place(lax.rem(my_row + k, rows)), me).start()

    @pl.loop(1, rows)
    def _(k):
        other = row_place(lax.rem(my_row + k, rows))
        name_copy(other, other).wait_recv()

    bring_names = pltpu.make_async_copy(names.at[pl.ds(my_tile * rows, rows)], row_scalars, local_sem)
    bring_names.start()
    bring_names.wait()

    def block_copy(peer, slot):
        return pltpu.make_async_remote_copy(
            src_ref=ask_packed.at[peer], dst_ref=blocks.at[slot], send_sem=block_send.at[peer], recv_sem=block_recv.at[slot],
            device_id=place(row_place(peer), rows), device_id_type=MESH)

    def read(peer, spot):
        return factors[jnp.maximum(row_scalars[peer, 0, my_row * CAP + spot], 0)].astype(jnp.bfloat16)

    @pl.loop(1, rows, unroll=True)
    def _(k):
        peer = lax.rem(my_row + k, rows)
        for spot in range(CAP):
            ask_packed[peer, spot] = read(peer, spot)
        block_copy(peer, my_row).start()

    for spot in range(CAP):
        blocks[my_row, spot] = read(my_row, spot)

    @pl.loop(1, tiles)
    def _(j):
        @pl.loop(0, rows)
        def _(k):
            name_copy(far_place(j, k), me).start()

    @pl.loop(1, rows)
    def _(k):
        peer = lax.rem(my_row + k, rows)
        block_copy(peer, peer).wait_recv()

    edge = TILE
    chunk = 256
    group = chunk // edge
    buffers = ((ab_even, cd_even, misfit_even), (ab_odd, cd_odd, misfit_odd))

    def block(slot, mode):
        index = spot_ref[0, mode * slots + slot]
        return blocks[index // CAP, lax.rem(index, CAP)].astype(jnp.float32)

    def work(slot, parity, before):
        if slot is not None:
            tile_copy(slot).wait()
            pair_ab, pair_cd, misfit = buffers[parity]
            one, two, three, four = (block(slot, mode) for mode in range(4))
            for part in range(edge // group):
                lines = slice(part * group, (part + 1) * group)
                at = pl.ds(part * chunk, chunk)
                pair_ab[at, :] = (one[lines][:, None, :] * two[None, :, :]).reshape(chunk, rank).astype(jnp.bfloat16)
                pair_cd[at, :] = (three[lines][:, None, :] * four[None, :, :]).reshape(chunk, rank).astype(jnp.bfloat16)
            second = jnp.zeros((edge, rank), jnp.float32)
        if before is not None:
            old_ab, _, old_misfit = buffers[1 - parity]
            old_three, old_four = block(before, 2), block(before, 3)
            fourth = jnp.zeros((edge, rank), jnp.float32)
        for part in range(edge // group):
            lines = slice(part * group, (part + 1) * group)
            at = pl.ds(part * chunk, chunk)
            if before is not None:
                right = lax.dot_general(old_misfit[:, at], old_ab[...], (((0,), (0,)), ((), ())), preferred_element_type=jnp.float32)
                right = right.reshape(group, edge, rank)
                grads[before * 4 + 2, lines, :] = jnp.sum(right * old_four[None, :, :], axis=1)
                fourth = fourth + jnp.sum(right * old_three[lines][:, None, :], axis=0)
            if slot is not None:
                model = lax.dot_general(pair_ab[at, :], pair_cd[...], (((1,), (1,)), ((), ())), preferred_element_type=jnp.float32)
                off = jnp.clip(model - stack[slot, at, :].astype(jnp.float32), -1.0, 1.0).astype(jnp.bfloat16)
                misfit[at, :] = off
                left = jnp.dot(off, pair_cd[...], preferred_element_type=jnp.float32).reshape(group, edge, rank)
                grads[slot * 4, lines, :] = jnp.sum(left * two[None, :, :], axis=1)
                second = second + jnp.sum(left * one[lines][:, None, :], axis=0)
        if slot is not None:
            grads[slot * 4 + 1] = second
        if before is not None:
            grads[before * 4 + 3] = fourth

    work(0, 0, None)

    @pl.loop(0, (slots - 1) // 2)
    def _(i):
        work(2 * i + 1, 1, 2 * i)
        work(2 * i + 2, 0, 2 * i + 1)

    if slots % 2 == 0:
        work(slots - 1, 1, slots - 2)
    work(None, slots % 2, slots - 1)

    share = TILE // tiles
    span = CAP * share
    total = factors.shape[0] * share

    def message(other, slot):
        return pltpu.make_async_remote_copy(
            src_ref=packed.at[other], dst_ref=landed.at[slot], send_sem=send_sem.at[other], recv_sem=recv_sem.at[slot],
            device_id=place(other, rows), device_id_type=MESH)

    @pl.loop(0, rows)
    def _(k):
        owner = lax.rem(my_row + k, rows)
        found = []
        for spot in range(CAP):
            index = inverse_ref[0, owner * CAP + spot]
            found.append(jnp.where(index >= 0, grads[jnp.maximum(index, 0)], 0.0))
        for tile in range(tiles):
            lines = slice(tile * share, (tile + 1) * share)
            packed[tile * rows + owner] = jnp.concatenate([piece[lines] for piece in found], axis=0).astype(jnp.bfloat16)

        for j in range(1, tiles):
            message(lax.rem(my_tile + j, tiles) * rows + owner, me).start()

        @pl.when(k > 0)
        def _():
            message(row_place(owner), me).start()

    landed[me] = packed[me]

    @pl.loop(1, tiles)
    def _(j):
        @pl.loop(0, rows)
        def _(k):
            other = far_place(j, k)
            name_copy(other, other).wait_recv()

    bring_all = pltpu.make_async_copy(names, name_scalars, local_sem)
    bring_all.start()
    bring_all.wait()
    inside = lax.broadcasted_iota(jnp.int32, (span, LANES), 0)

    @pl.loop(0, peers)
    def _(source):
        base = jnp.zeros((span, LANES), jnp.int32)
        for spot in range(CAP):
            name = name_scalars[source, 0, my_row * CAP + spot]
            line = jnp.where(name >= 0, name * share - spot * share, -(1 << 20))
            base = jnp.where(inside // share == spot, line, base)
        target[pl.ds(source * span, span), :] = base + inside

    marks = [
        jnp.where(target[...] == lax.broadcasted_iota(jnp.int32, (peers * span, LANES), 1) + at, 1.0, 0.0).astype(jnp.bfloat16)
        for at in range(0, total, LANES)
    ]

    @pl.loop(1, peers)
    def _(k):
        other = lax.rem(me + k, peers)
        message(other, other).wait_recv()

    everything = landed[...].reshape(peers * span, rank)
    for at, mark in zip(range(0, total, LANES), marks):
        size = min(LANES, total - at)
        summed = lax.dot_general(mark, everything, (((0,), (0,)), ((), ())), preferred_element_type=jnp.float32)
        gathered[my_tile, pl.ds(at, size), :] = summed[:size].astype(jnp.bfloat16)

    def spread(towards, share_at, sems):
        return pltpu.make_async_remote_copy(
            src_ref=gathered.at[share_at], dst_ref=gathered.at[share_at], send_sem=sems.at[share_at], recv_sem=all_recv.at[share_at],
            device_id=place(towards * rows + my_row, rows), device_id_type=MESH)

    def each_way(tile, act):
        @pl.when((tile <= my_tile) & (my_tile + 1 < tiles))
        def _():
            act(spread(my_tile + 1, tile, up_send))

        @pl.when((tile >= my_tile) & (my_tile > 0))
        def _():
            act(spread(my_tile - 1, tile, down_send))

    per = 16 // share

    def finished(tile):
        lines = pl.ds(pl.multiple_of(tile * share, share), share)
        return pltpu.make_async_copy(factors.at[:, lines, :], out_hbm.at[:, lines, :], out_sem.at[tile])

    def update(tile):
        if share % 8:
            return
        lines = pl.ds(pl.multiple_of(tile * share, share), share)
        for at in range(0, total, 16):
            values = gathered[tile, pl.ds(at, 16), :].astype(jnp.float32)
            for piece in range(per):
                name = at // share + piece
                factors[name, lines, :] = factors[name, lines, :] - step_size * values[piece * share:(piece + 1) * share]
        finished(tile).start()

    each_way(my_tile, lambda copy: copy.start())
    update(my_tile)

    for away in range(1, tiles):
        for tile, inside_chain in ((my_tile - away, my_tile >= away), (my_tile + away, my_tile + away < tiles)):
            @pl.when(inside_chain)
            def _():
                spread(my_tile, tile, up_send).wait_recv()
                each_way(tile, lambda copy: copy.start())
                update(tile)

    if share % 8:
        for at in range(0, total, 16):
            values = [gathered[tile, pl.ds(at, 16), :].astype(jnp.float32) for tile in range(tiles)]
            for piece in range(per):
                name = at // share + piece
                whole = jnp.concatenate([value[piece * share:(piece + 1) * share] for value in values], axis=0)
                factors[name] = factors[name] - step_size * whole
        write = pltpu.make_async_copy(factors, out_hbm, local_sem)
        write.start()
        write.wait()
    else:
        @pl.loop(0, tiles)
        def _(tile):
            finished(tile).wait()

    @pl.loop(0, tiles)
    def _(tile):
        each_way(tile, lambda copy: copy.wait_send())

    @pl.loop(1, rows)
    def _(k):
        peer = lax.rem(my_row + k, rows)
        block_copy(peer, my_row).wait_send()

    @pl.loop(1, peers)
    def _(k):
        other = lax.rem(me + k, peers)
        name_copy(other, me).wait_send()
        message(other, me).wait_send()


def step(spot, inverse, want, tile_stack, factors, tiles, rows):
    peers = tiles * rows
    slots, height, width = tile_stack.shape
    local, edge, rank = factors.shape
    share = TILE // tiles
    span = CAP * share
    dma = lambda *shape: pltpu.SemaphoreType.DMA(shape)
    bf16 = lambda *shape: pltpu.VMEM(shape, jnp.bfloat16)
    return pl.pallas_call(
        functools.partial(step_kernel, tiles, rows),
        out_shape=jax.ShapeDtypeStruct((local, edge, rank), jnp.float32),
        in_specs=[pl.BlockSpec(memory_space=pltpu.SMEM)] * 2 + [pl.BlockSpec(memory_space=pltpu.VMEM)] + [pl.BlockSpec(memory_space=pl.ANY)] * 2,
        out_specs=pl.BlockSpec(memory_space=pl.ANY),
        scratch_shapes=[
            pltpu.VMEM((local, edge, rank), jnp.float32),
            bf16(slots, height, width),
            pltpu.VMEM((peers, 1, LANES), jnp.int32),
            pltpu.SMEM((peers, 1, LANES), jnp.int32),
            pltpu.SMEM((rows, 1, LANES), jnp.int32),
            bf16(rows, CAP, TILE, rank),
            bf16(rows, CAP, TILE, rank),
            bf16(height, rank), bf16(height, rank), bf16(width, rank), bf16(width, rank),
            bf16(height, width), bf16(height, width),
            pltpu.VMEM((slots * 4, TILE, rank), jnp.float32),
            bf16(peers, span, rank),
            bf16(peers, span, rank),
            pltpu.VMEM((peers * span, LANES), jnp.int32),
            bf16(tiles, local * share, rank),
            dma(peers), dma(peers), dma(rows), dma(rows), dma(peers), dma(peers),
            dma(tiles), dma(tiles), dma(tiles), dma(slots), dma(tiles), pltpu.SemaphoreType.DMA,
        ],
        compiler_params=pltpu.CompilerParams(collective_id=0, has_side_effects=True, vmem_limit_bytes=56 << 20),
        cost_estimate=pl.CostEstimate(flops=6 * slots * height * width * rank, bytes_accessed=2 * slots * height * width, transcendentals=0),
        name="gradient_step",
    )(spot, inverse, want, tile_stack, factors)


def tables(coords, live_count, local_blocks):
    slots = coords.shape[0]
    names = slots * 4
    flat = coords.T.reshape(names)
    owner = flat // local_blocks
    order = jnp.arange(names)
    live = order % slots < live_count
    earlier = (owner[None, :] == owner[:, None]) & live[None, :] & (order[None, :] < order[:, None])
    spot = owner * CAP + jnp.sum(earlier.astype(jnp.int32), axis=1)
    spot = jnp.where(live, spot, -1)
    hit = spot[None, :] == jnp.arange(LANES)[:, None]
    block = (order // slots) * local_blocks + flat - owner * local_blocks
    want = jnp.max(jnp.where(hit, block[None, :], -1), axis=1)
    inverse = jnp.max(jnp.where(hit, ((order % slots) * 4 + order // slots)[None, :], -1), axis=1)
    return jnp.maximum(spot, 0).reshape(1, names), want.reshape(1, LANES), inverse.reshape(1, LANES)


def on_device(tile_values, tile_coords, tile_count, factors):
    tiles, rows = lax.axis_size("tiles"), lax.axis_size("rows")
    modes, local_rows, rank = factors.shape
    spot, want, inverse = tables(tile_coords[0], tile_count[0], local_rows // TILE)
    updated = step(spot, inverse, want, tile_values[0], factors.reshape(-1, TILE, rank), tiles, rows)
    return updated.reshape(factors.shape)


def solution(mesh):
    return jax.shard_map(
        on_device,
        mesh=mesh,
        in_specs=(
            P(("tiles", "rows"), None, None, None),
            P(("tiles", "rows"), None, None),
            P(("tiles", "rows")),
            P(None, "rows", None),
        ),
        out_specs=P(None, "rows", None),
        check_vma=False,
    )
```

```python
import functools

import jax
import jax.numpy as jnp
from jax import lax
from jax.experimental import pallas as pl
from jax.experimental.pallas import tpu as pltpu
from jax.sharding import PartitionSpec as P

TILE = 32
CAP = 4
LANES = 128
MESH = pl.DeviceIdType.MESH

step_size = 0.02


def place(index, rows):
    return {"tiles": index // rows, "rows": lax.rem(index, rows)}


def step_kernel(
    tiles, rows, spot_ref, inverse_ref, want_ref, tile_hbm, factors_hbm, out_ref,
    factors, stack, names, name_scalars, row_scalars, ask_packed, blocks, pair_ab, pair_cd, misfit,
    grads, packed, landed, target, gathered,
    name_send, name_recv, block_send, block_recv, send_sem, recv_sem, up_send, down_send, all_recv, tile_sem, local_sem,
):
    peers = tiles * rows
    my_tile, my_row = lax.axis_index("tiles"), lax.axis_index("rows")
    me = my_tile * rows + my_row
    slots = stack.shape[0]
    rank = factors.shape[2]
    row_place = lambda peer: my_tile * rows + peer
    far_place = lambda j, k: lax.rem(my_tile + j, tiles) * rows + lax.rem(my_row + k, rows)

    bring_factors = pltpu.make_async_copy(factors_hbm, factors, local_sem)
    bring_factors.start()
    barrier = pltpu.get_barrier_semaphore()
    for j in range(tiles):
        @pl.loop(0 if j else 1, rows, unroll=True)
        def _(k):
            pl.semaphore_signal(barrier, inc=1, device_id=place(far_place(j, k), rows), device_id_type=MESH)

    def tile_copy(slot):
        return pltpu.make_async_copy(tile_hbm.at[slot], stack.at[slot], tile_sem.at[slot])

    names[me] = want_ref[...]
    bring_factors.wait()
    pl.semaphore_wait(barrier, peers - 1)

    def name_copy(other, slot):
        return pltpu.make_async_remote_copy(
            src_ref=want_ref, dst_ref=names.at[slot], send_sem=name_send.at[other], recv_sem=name_recv.at[slot],
            device_id=place(other, rows), device_id_type=MESH)

    @pl.loop(1, rows, unroll=True)
    def _(k):
        name_copy(row_place(lax.rem(my_row + k, rows)), me).start()

    @pl.loop(1, rows)
    def _(k):
        other = row_place(lax.rem(my_row + k, rows))
        name_copy(other, other).wait_recv()

    bring_names = pltpu.make_async_copy(names.at[pl.ds(my_tile * rows, rows)], row_scalars, local_sem)
    bring_names.start()
    bring_names.wait()

    def block_copy(peer, slot):
        return pltpu.make_async_remote_copy(
            src_ref=ask_packed.at[peer], dst_ref=blocks.at[slot], send_sem=block_send.at[peer], recv_sem=block_recv.at[slot],
            device_id=place(row_place(peer), rows), device_id_type=MESH)

    def read(peer, spot):
        return factors[jnp.maximum(row_scalars[peer, 0, my_row * CAP + spot], 0)].astype(jnp.bfloat16)

    @pl.loop(1, rows, unroll=True)
    def _(k):
        peer = lax.rem(my_row + k, rows)
        for spot in range(CAP):
            ask_packed[peer, spot] = read(peer, spot)
        block_copy(peer, my_row).start()

    for spot in range(CAP):
        blocks[my_row, spot] = read(my_row, spot)

    @pl.loop(1, tiles)
    def _(j):
        @pl.loop(0, rows)
        def _(k):
            name_copy(far_place(j, k), me).start()

    tile_copy(0).start()
    tile_copy(1).start()

    @pl.loop(1, rows)
    def _(k):
        peer = lax.rem(my_row + k, rows)
        block_copy(peer, peer).wait_recv()

    edge = TILE
    chunk = 256
    group = chunk // edge
    def block(slot, mode):
        index = spot_ref[slot * 4 + mode]
        return blocks[index // CAP, lax.rem(index, CAP)].astype(jnp.float32)

    @pl.loop(0, slots)
    def _(slot):
        @pl.when(slot + 2 < slots)
        def _():
            tile_copy(slot + 2).start()

        one, two, three, four = (block(slot, mode) for mode in range(4))
        for part in range(edge // group):
            lines = slice(part * group, (part + 1) * group)
            at = pl.ds(part * chunk, chunk)
            pair_ab[at, :] = (one[lines][:, None, :] * two[None, :, :]).reshape(chunk, rank).astype(jnp.bfloat16)
            pair_cd[at, :] = (three[lines][:, None, :] * four[None, :, :]).reshape(chunk, rank).astype(jnp.bfloat16)
        tile_copy(slot).wait()
        second = jnp.zeros((edge, rank), jnp.float32)
        for part in range(edge // group):
            lines = slice(part * group, (part + 1) * group)
            at = pl.ds(part * chunk, chunk)
            model = lax.dot_general(pair_ab[at, :], pair_cd[...], (((1,), (1,)), ((), ())), preferred_element_type=jnp.float32)
            off = jnp.clip(model - stack[slot, at, :].astype(jnp.float32), -1.0, 1.0).astype(jnp.bfloat16)
            misfit[at, :] = off
            left = jnp.dot(off, pair_cd[...], preferred_element_type=jnp.float32).reshape(group, edge, rank)
            grads[slot * 4, lines, :] = jnp.sum(left * two[None, :, :], axis=1)
            second = second + jnp.sum(left * one[lines][:, None, :], axis=0)
        grads[slot * 4 + 1] = second
        fourth = jnp.zeros((edge, rank), jnp.float32)
        for part in range(edge // group):
            lines = slice(part * group, (part + 1) * group)
            at = pl.ds(part * chunk, chunk)
            right = lax.dot_general(misfit[:, at], pair_ab[...], (((0,), (0,)), ((), ())), preferred_element_type=jnp.float32)
            right = right.reshape(group, edge, rank)
            grads[slot * 4 + 2, lines, :] = jnp.sum(right * four[None, :, :], axis=1)
            fourth = fourth + jnp.sum(right * three[lines][:, None, :], axis=0)
        grads[slot * 4 + 3] = fourth

    share = TILE // tiles
    span = CAP * share
    total = factors.shape[0] * share

    def message(other, slot):
        return pltpu.make_async_remote_copy(
            src_ref=packed.at[other], dst_ref=landed.at[slot], send_sem=send_sem.at[other], recv_sem=recv_sem.at[slot],
            device_id=place(other, rows), device_id_type=MESH)

    @pl.loop(0, rows)
    def _(k):
        owner = lax.rem(my_row + k, rows)
        found = []
        for spot in range(CAP):
            index = inverse_ref[0, owner * CAP + spot]
            found.append(jnp.where(index >= 0, grads[jnp.maximum(index, 0)], 0.0))
        for tile in range(tiles):
            lines = slice(tile * share, (tile + 1) * share)
            packed[tile * rows + owner] = jnp.concatenate([piece[lines] for piece in found], axis=0).astype(jnp.bfloat16)

        for j in range(1, tiles):
            message(lax.rem(my_tile + j, tiles) * rows + owner, me).start()

        @pl.when(k > 0)
        def _():
            message(row_place(owner), me).start()

    landed[me] = packed[me]

    @pl.loop(1, tiles)
    def _(j):
        @pl.loop(0, rows)
        def _(k):
            other = far_place(j, k)
            name_copy(other, other).wait_recv()

    bring_all = pltpu.make_async_copy(names, name_scalars, local_sem)
    bring_all.start()
    bring_all.wait()
    inside = lax.broadcasted_iota(jnp.int32, (span, LANES), 0)

    @pl.loop(0, peers)
    def _(source):
        base = jnp.zeros((span, LANES), jnp.int32)
        for spot in range(CAP):
            name = name_scalars[source, 0, my_row * CAP + spot]
            line = jnp.where(name >= 0, name * share - spot * share, -(1 << 20))
            base = jnp.where(inside // share == spot, line, base)
        target[pl.ds(source * span, span), :] = base + inside

    marks = [
        jnp.where(target[...] == lax.broadcasted_iota(jnp.int32, (peers * span, LANES), 1) + at, 1.0, 0.0).astype(jnp.bfloat16)
        for at in range(0, total, LANES)
    ]

    @pl.loop(1, peers)
    def _(k):
        other = lax.rem(me + k, peers)
        message(other, other).wait_recv()

    everything = landed[...].reshape(peers * span, rank)
    for at, mark in zip(range(0, total, LANES), marks):
        size = min(LANES, total - at)
        summed = lax.dot_general(mark, everything, (((0,), (0,)), ((), ())), preferred_element_type=jnp.float32)
        gathered[my_tile, pl.ds(at, size), :] = summed[:size].astype(jnp.bfloat16)

    def spread(towards, share_at, sems):
        return pltpu.make_async_remote_copy(
            src_ref=gathered.at[share_at], dst_ref=gathered.at[share_at], send_sem=sems.at[share_at], recv_sem=all_recv.at[share_at],
            device_id=place(towards * rows + my_row, rows), device_id_type=MESH)

    def each_way(tile, act):
        @pl.when((tile <= my_tile) & (my_tile + 1 < tiles))
        def _():
            act(spread(my_tile + 1, tile, up_send))

        @pl.when((tile >= my_tile) & (my_tile > 0))
        def _():
            act(spread(my_tile - 1, tile, down_send))

    per = 16 // share

    def update(tile):
        if share % 8:
            return
        lines = pl.ds(pl.multiple_of(tile * share, share), share)

        @pl.loop(0, total // 16, unroll=4)
        def _(i):
            values = gathered[tile, pl.ds(pl.multiple_of(i * 16, 16), 16), :].astype(jnp.float32)
            for piece in range(per):
                name = i * per + piece
                out_ref[name, lines, :] = factors[name, lines, :] - step_size * values[piece * share:(piece + 1) * share]

    each_way(my_tile, lambda copy: copy.start())
    update(my_tile)

    for away in range(1, tiles):
        both = ((my_tile - away, my_tile >= away), (my_tile + away, my_tile + away < tiles))
        for tile, inside_chain in both:
            @pl.when(inside_chain)
            def _():
                spread(my_tile, tile, up_send).wait_recv()
                each_way(tile, lambda copy: copy.start())

        for tile, inside_chain in both:
            @pl.when(inside_chain)
            def _():
                update(tile)

    if share % 8:
        for at in range(0, total, 16):
            values = [gathered[tile, pl.ds(at, 16), :].astype(jnp.float32) for tile in range(tiles)]
            for piece in range(per):
                name = at // share + piece
                whole = jnp.concatenate([value[piece * share:(piece + 1) * share] for value in values], axis=0)
                out_ref[name] = factors[name] - step_size * whole

    @pl.loop(0, tiles)
    def _(tile):
        each_way(tile, lambda copy: copy.wait_send())

    @pl.loop(1, rows)
    def _(k):
        peer = lax.rem(my_row + k, rows)
        block_copy(peer, my_row).wait_send()

    @pl.loop(1, peers)
    def _(k):
        other = lax.rem(me + k, peers)
        name_copy(other, me).wait_send()
        message(other, me).wait_send()


def step(spot, inverse, want, tile_stack, factors, tiles, rows):
    peers = tiles * rows
    slots, height, width = tile_stack.shape
    local, edge, rank = factors.shape
    share = TILE // tiles
    span = CAP * share
    dma = lambda *shape: pltpu.SemaphoreType.DMA(shape)
    bf16 = lambda *shape: pltpu.VMEM(shape, jnp.bfloat16)
    return pl.pallas_call(
        functools.partial(step_kernel, tiles, rows),
        out_shape=jax.ShapeDtypeStruct((local, edge, rank), jnp.float32),
        in_specs=[pl.BlockSpec(memory_space=pltpu.SMEM)] * 2 + [pl.BlockSpec(memory_space=pltpu.VMEM)] + [pl.BlockSpec(memory_space=pltpu.HBM)] * 2,
        out_specs=pl.BlockSpec(memory_space=pltpu.VMEM),
        scratch_shapes=[
            pltpu.VMEM((local, edge, rank), jnp.float32),
            bf16(slots, height, width),
            pltpu.VMEM((peers, 1, LANES), jnp.int32),
            pltpu.SMEM((peers, 1, LANES), jnp.int32),
            pltpu.SMEM((rows, 1, LANES), jnp.int32),
            bf16(rows, CAP, TILE, rank),
            bf16(rows, CAP, TILE, rank),
            bf16(height, rank), bf16(width, rank), bf16(height, width),
            pltpu.VMEM((slots * 4, TILE, rank), jnp.float32),
            bf16(peers, span, rank),
            bf16(peers, span, rank),
            pltpu.VMEM((peers * span, LANES), jnp.int32),
            bf16(tiles, local * share, rank),
            dma(peers), dma(peers), dma(rows), dma(rows), dma(peers), dma(peers),
            dma(tiles), dma(tiles), dma(tiles), dma(slots), pltpu.SemaphoreType.DMA,
        ],
        compiler_params=pltpu.CompilerParams(collective_id=0, has_side_effects=True, vmem_limit_bytes=40 << 20),
        cost_estimate=pl.CostEstimate(flops=6 * slots * height * width * rank, bytes_accessed=2 * slots * height * width, transcendentals=0),
        name="gradient_step",
    )(spot, inverse, want, tile_stack, factors)


def tables(coords, live_count, local_blocks):
    slots = coords.shape[0]
    names = slots * 4
    flat = coords.reshape(names)
    owner = flat // local_blocks
    order = jnp.arange(names)
    live = order // 4 < live_count
    earlier = (owner[None, :] == owner[:, None]) & live[None, :] & (order[None, :] < order[:, None])
    spot = owner * CAP + jnp.sum(earlier.astype(jnp.int32), axis=1)
    spot = jnp.where(live, spot, -1)
    hit = spot[None, :] == jnp.arange(LANES)[:, None]
    block = (order % 4) * local_blocks + flat - owner * local_blocks
    want = jnp.max(jnp.where(hit, block[None, :], -1), axis=1)
    inverse = jnp.max(jnp.where(hit, order[None, :], -1), axis=1)
    return jnp.maximum(spot, 0), want.reshape(1, LANES), inverse.reshape(1, LANES)


def on_device(tile_values, tile_coords, tile_count, factors):
    tiles, rows = lax.axis_size("tiles"), lax.axis_size("rows")
    modes, local_rows, rank = factors.shape
    spot, want, inverse = tables(tile_coords[0], tile_count[0], local_rows // TILE)
    updated = step(spot, inverse, want, tile_values[0], factors.reshape(-1, TILE, rank), tiles, rows)
    return updated.reshape(factors.shape)


def solution(mesh):
    return jax.shard_map(
        on_device,
        mesh=mesh,
        in_specs=(
            P(("tiles", "rows"), None, None, None),
            P(("tiles", "rows"), None, None),
            P(("tiles", "rows")),
            P(None, "rows", None),
        ),
        out_specs=P(None, "rows", None),
        check_vma=False,
    )
```

```python
import functools

import jax
import jax.numpy as jnp
from jax import lax
from jax.experimental import pallas as pl
from jax.experimental.pallas import tpu as pltpu
from jax.sharding import PartitionSpec as P

TILE = 32
CAP = 4
LANES = 128
MESH = pl.DeviceIdType.MESH

step_size = 0.02


def place(index, rows):
    return {"tiles": index // rows, "rows": lax.rem(index, rows)}


def step_kernel(
    tiles, rows, spot_ref, inverse_ref, want_ref, tile_hbm, factors, out_ref,
    stack, names, name_scalars, row_scalars, ask_packed, blocks, pair_ab, pair_cd, misfit,
    grads, packed, landed, target, gathered,
    name_send, name_recv, block_send, block_recv, send_sem, recv_sem, direct_send, relay_send, all_recv, tile_sem, local_sem,
):
    peers = tiles * rows
    my_tile, my_row = lax.axis_index("tiles"), lax.axis_index("rows")
    me = my_tile * rows + my_row
    slots = stack.shape[0]
    rank = factors.shape[2]
    row_place = lambda peer: my_tile * rows + peer
    far_place = lambda j, k: lax.rem(my_tile + j, tiles) * rows + lax.rem(my_row + k, rows)

    barrier = pltpu.get_barrier_semaphore()
    for j in range(tiles):
        @pl.loop(0 if j else 1, rows, unroll=True)
        def _(k):
            pl.semaphore_signal(barrier, inc=1, device_id=place(far_place(j, k), rows), device_id_type=MESH)

    def tile_copy(slot):
        return pltpu.make_async_copy(tile_hbm.at[slot], stack.at[slot], tile_sem.at[slot])

    names[me] = want_ref[...]
    pl.semaphore_wait(barrier, peers - 1)

    def name_copy(other, slot):
        return pltpu.make_async_remote_copy(
            src_ref=want_ref, dst_ref=names.at[slot], send_sem=name_send.at[other], recv_sem=name_recv.at[slot],
            device_id=place(other, rows), device_id_type=MESH)

    @pl.loop(1, rows, unroll=True)
    def _(k):
        name_copy(row_place(lax.rem(my_row + k, rows)), me).start()

    @pl.loop(1, rows)
    def _(k):
        other = row_place(lax.rem(my_row + k, rows))
        name_copy(other, other).wait_recv()

    bring_names = pltpu.make_async_copy(names.at[pl.ds(my_tile * rows, rows)], row_scalars, local_sem)
    bring_names.start()
    bring_names.wait()

    def block_copy(peer, slot):
        return pltpu.make_async_remote_copy(
            src_ref=ask_packed.at[peer], dst_ref=blocks.at[slot], send_sem=block_send.at[peer], recv_sem=block_recv.at[slot],
            device_id=place(row_place(peer), rows), device_id_type=MESH)

    def read(peer, spot):
        return factors[jnp.maximum(row_scalars[peer, 0, my_row * CAP + spot], 0)].astype(jnp.bfloat16)

    @pl.loop(1, rows, unroll=True)
    def _(k):
        peer = lax.rem(my_row + k, rows)
        for spot in range(CAP):
            ask_packed[peer, spot] = read(peer, spot)
        block_copy(peer, my_row).start()

    for spot in range(CAP):
        blocks[my_row, spot] = read(my_row, spot)

    @pl.loop(1, tiles)
    def _(j):
        @pl.loop(0, rows)
        def _(k):
            name_copy(far_place(j, k), me).start()

    tile_copy(0).start()
    tile_copy(1).start()

    @pl.loop(1, rows)
    def _(k):
        peer = lax.rem(my_row + k, rows)
        block_copy(peer, peer).wait_recv()

    edge = TILE
    chunk = 256
    group = chunk // edge
    def block(slot, mode):
        index = spot_ref[mode, slot]
        return blocks[index // CAP, lax.rem(index, CAP)].astype(jnp.float32)

    @pl.loop(0, slots)
    def _(slot):
        @pl.when(slot + 2 < slots)
        def _():
            tile_copy(slot + 2).start()

        one, two, three, four = (block(slot, mode) for mode in range(4))
        for part in range(edge // group):
            lines = slice(part * group, (part + 1) * group)
            at = pl.ds(part * chunk, chunk)
            pair_ab[at, :] = (one[lines][:, None, :] * two[None, :, :]).reshape(chunk, rank).astype(jnp.bfloat16)
            pair_cd[at, :] = (three[lines][:, None, :] * four[None, :, :]).reshape(chunk, rank).astype(jnp.bfloat16)
        tile_copy(slot).wait()
        second = jnp.zeros((edge, rank), jnp.float32)
        for part in range(edge // group):
            lines = slice(part * group, (part + 1) * group)
            at = pl.ds(part * chunk, chunk)
            model = lax.dot_general(pair_ab[at, :], pair_cd[...], (((1,), (1,)), ((), ())), preferred_element_type=jnp.float32)
            off = jnp.clip(model - stack[slot, at, :].astype(jnp.float32), -1.0, 1.0).astype(jnp.bfloat16)
            misfit[at, :] = off
            left = jnp.dot(off, pair_cd[...], preferred_element_type=jnp.float32).reshape(group, edge, rank)
            grads[slot * 4, lines, :] = jnp.sum(left * two[None, :, :], axis=1)
            second = second + jnp.sum(left * one[lines][:, None, :], axis=0)
        grads[slot * 4 + 1] = second
        fourth = jnp.zeros((edge, rank), jnp.float32)
        for part in range(edge // group):
            lines = slice(part * group, (part + 1) * group)
            at = pl.ds(part * chunk, chunk)
            right = lax.dot_general(misfit[:, at], pair_ab[...], (((0,), (0,)), ((), ())), preferred_element_type=jnp.float32)
            right = right.reshape(group, edge, rank)
            grads[slot * 4 + 2, lines, :] = jnp.sum(right * four[None, :, :], axis=1)
            fourth = fourth + jnp.sum(right * three[lines][:, None, :], axis=0)
        grads[slot * 4 + 3] = fourth

    share = TILE // tiles
    span = CAP * share
    total = factors.shape[0] * share

    def message(other, slot):
        return pltpu.make_async_remote_copy(
            src_ref=packed.at[other], dst_ref=landed.at[slot], send_sem=send_sem.at[other], recv_sem=recv_sem.at[slot],
            device_id=place(other, rows), device_id_type=MESH)

    @pl.loop(0, rows)
    def _(k):
        owner = lax.rem(my_row + k, rows)
        found = []
        for spot in range(CAP):
            index = inverse_ref[0, owner * CAP + spot]
            found.append(jnp.where(index >= 0, grads[jnp.maximum(index, 0)], 0.0))
        for tile in range(tiles):
            lines = slice(tile * share, (tile + 1) * share)
            packed[tile * rows + owner] = jnp.concatenate([piece[lines] for piece in found], axis=0).astype(jnp.bfloat16)

        for j in range(1, tiles):
            message(lax.rem(my_tile + j, tiles) * rows + owner, me).start()

        @pl.when(k > 0)
        def _():
            message(row_place(owner), me).start()

    landed[me] = packed[me]

    @pl.loop(1, tiles)
    def _(j):
        @pl.loop(0, rows)
        def _(k):
            other = far_place(j, k)
            name_copy(other, other).wait_recv()

    bring_all = pltpu.make_async_copy(names, name_scalars, local_sem)
    bring_all.start()
    bring_all.wait()
    inside = lax.broadcasted_iota(jnp.int32, (span, LANES), 0)

    @pl.loop(0, peers)
    def _(source):
        base = jnp.zeros((span, LANES), jnp.int32)
        for spot in range(CAP):
            name = name_scalars[source, 0, my_row * CAP + spot]
            line = jnp.where(name >= 0, name * share - spot * share, -(1 << 20))
            base = jnp.where(inside // share == spot, line, base)
        target[pl.ds(source * span, span), :] = base + inside

    marks = [
        jnp.where(target[...] == lax.broadcasted_iota(jnp.int32, (peers * span, LANES), 1) + at, 1.0, 0.0).astype(jnp.bfloat16)
        for at in range(0, total, LANES)
    ]

    @pl.loop(1, peers)
    def _(k):
        other = lax.rem(me + k, peers)
        message(other, other).wait_recv()

    everything = landed[...].reshape(peers * span, rank)
    for at, mark in zip(range(0, total, LANES), marks):
        size = min(LANES, total - at)
        summed = lax.dot_general(mark, everything, (((0,), (0,)), ((), ())), preferred_element_type=jnp.float32)
        gathered[my_tile, pl.ds(at, size), :] = summed[:size].astype(jnp.bfloat16)

    def spread(towards, share_at, sems):
        return pltpu.make_async_remote_copy(
            src_ref=gathered.at[share_at], dst_ref=gathered.at[share_at], send_sem=sems, recv_sem=all_recv.at[share_at],
            device_id=place(towards * rows + my_row, rows), device_id_type=MESH)

    last = tiles - 1

    def each_direct(act):
        for away in range(last - 1, 0, -1):
            @pl.when(my_tile + away < tiles)
            def _():
                act(spread(my_tile + away, my_tile, direct_send.at[my_tile + away]))

            @pl.when(my_tile >= away)
            def _():
                act(spread(my_tile - away, my_tile, direct_send.at[my_tile - away]))

    def each_relay(tile, act):
        @pl.when((tile == 0) & (my_tile == last - 1))
        def _():
            act(spread(last, 0, relay_send.at[0]))

        @pl.when((tile == last) & (my_tile == 1))
        def _():
            act(spread(0, last, relay_send.at[1]))

    per = 16 // share

    def update(tile):
        if share % 8:
            return
        lines = pl.ds(pl.multiple_of(tile * share, share), share)

        @pl.loop(0, total // 16, unroll=4)
        def _(i):
            values = gathered[tile, pl.ds(pl.multiple_of(i * 16, 16), 16), :].astype(jnp.float32)
            for piece in range(per):
                name = i * per + piece
                out_ref[name, lines, :] = factors[name, lines, :] - step_size * values[piece * share:(piece + 1) * share]

    each_direct(lambda copy: copy.start())
    update(my_tile)

    for away in (2, 1) + tuple(range(3, tiles)):
        both = ((my_tile - away, my_tile >= away), (my_tile + away, my_tile + away < tiles))
        for tile, inside_chain in both:
            @pl.when(inside_chain)
            def _():
                spread(my_tile, tile, direct_send.at[my_tile]).wait_recv()
                each_relay(tile, lambda copy: copy.start())

        for tile, inside_chain in both:
            @pl.when(inside_chain)
            def _():
                update(tile)

    if share % 8:
        for at in range(0, total, 16):
            values = [gathered[tile, pl.ds(at, 16), :].astype(jnp.float32) for tile in range(tiles)]
            for piece in range(per):
                name = at // share + piece
                whole = jnp.concatenate([value[piece * share:(piece + 1) * share] for value in values], axis=0)
                out_ref[name] = factors[name] - step_size * whole

    each_direct(lambda copy: copy.wait_send())
    each_relay(0, lambda copy: copy.wait_send())
    each_relay(last, lambda copy: copy.wait_send())

    @pl.loop(1, rows)
    def _(k):
        peer = lax.rem(my_row + k, rows)
        block_copy(peer, my_row).wait_send()

    @pl.loop(1, peers)
    def _(k):
        other = lax.rem(me + k, peers)
        name_copy(other, me).wait_send()
        message(other, me).wait_send()


def step(spot, inverse, want, tile_stack, factors, tiles, rows):
    peers = tiles * rows
    slots, height, width = tile_stack.shape
    local, edge, rank = factors.shape
    share = TILE // tiles
    span = CAP * share
    dma = lambda *shape: pltpu.SemaphoreType.DMA(shape)
    bf16 = lambda *shape: pltpu.VMEM(shape, jnp.bfloat16)
    return pl.pallas_call(
        functools.partial(step_kernel, tiles, rows),
        out_shape=jax.ShapeDtypeStruct((local, edge, rank), jnp.float32),
        in_specs=[pl.BlockSpec(memory_space=pltpu.SMEM)] * 2 + [pl.BlockSpec(memory_space=pltpu.VMEM), pl.BlockSpec(memory_space=pl.ANY), pl.BlockSpec(memory_space=pltpu.VMEM)],
        out_specs=pl.BlockSpec(memory_space=pltpu.VMEM),
        scratch_shapes=[
            bf16(slots, height, width),
            pltpu.VMEM((peers, 1, LANES), jnp.int32),
            pltpu.SMEM((peers, 1, LANES), jnp.int32),
            pltpu.SMEM((rows, 1, LANES), jnp.int32),
            bf16(rows, CAP, TILE, rank),
            bf16(rows, CAP, TILE, rank),
            bf16(height, rank), bf16(width, rank), bf16(height, width),
            pltpu.VMEM((slots * 4, TILE, rank), jnp.float32),
            bf16(peers, span, rank),
            bf16(peers, span, rank),
            pltpu.VMEM((peers * span, LANES), jnp.int32),
            bf16(tiles, local * share, rank),
            dma(peers), dma(peers), dma(rows), dma(rows), dma(peers), dma(peers),
            dma(tiles), dma(2), dma(tiles), dma(slots), pltpu.SemaphoreType.DMA,
        ],
        compiler_params=pltpu.CompilerParams(collective_id=0, has_side_effects=True, vmem_limit_bytes=40 << 20),
        cost_estimate=pl.CostEstimate(flops=6 * slots * height * width * rank, bytes_accessed=2 * slots * height * width, transcendentals=0),
        name="gradient_step",
    )(spot, inverse, want, tile_stack, factors)


def tables(coords, live_count, local_blocks):
    flat = coords.T
    owner = flat // local_blocks
    mode = lax.broadcasted_iota(jnp.int32, flat.shape, 0)
    slot = lax.broadcasted_iota(jnp.int32, flat.shape, 1)
    order = slot * 4 + mode
    live = slot < live_count
    earlier = (owner == owner[:, :, None, None]) & live & (order < order[:, :, None, None])
    spot = owner * CAP + jnp.sum(earlier.astype(jnp.int32), axis=(2, 3))
    spot = jnp.where(live, spot, -1)
    hit = spot == jnp.arange(LANES)[:, None, None]
    block = mode * local_blocks + flat - owner * local_blocks
    want = jnp.max(jnp.where(hit, block, -1), axis=(1, 2))
    inverse = jnp.max(jnp.where(hit, order, -1), axis=(1, 2))
    return jnp.maximum(spot, 0), want.reshape(1, LANES), inverse.reshape(1, LANES)


def on_device(tile_values, tile_coords, tile_count, factors):
    tiles, rows = lax.axis_size("tiles"), lax.axis_size("rows")
    modes, local_rows, rank = factors.shape
    spot, want, inverse = tables(tile_coords[0], tile_count[0], local_rows // TILE)
    updated = step(spot, inverse, want, tile_values[0], factors.reshape(-1, TILE, rank), tiles, rows)
    return updated.reshape(factors.shape)


def solution(mesh):
    return jax.shard_map(
        on_device,
        mesh=mesh,
        in_specs=(
            P(("tiles", "rows"), None, None, None),
            P(("tiles", "rows"), None, None),
            P(("tiles", "rows")),
            P(None, "rows", None),
        ),
        out_specs=P(None, "rows", None),
        check_vma=False,
    )
```

```python
import functools

import jax
import jax.numpy as jnp
from jax import lax
from jax.experimental import pallas as pl
from jax.experimental.pallas import tpu as pltpu
from jax.sharding import PartitionSpec as P

TILE = 32
CAP = 4
LANES = 128
MESH = pl.DeviceIdType.MESH

step_size = 0.02


def place(index, rows):
    return {"tiles": index // rows, "rows": lax.rem(index, rows)}


def step_kernel(
    tiles, rows, spot_ref, inverse_ref, want_ref, tile_hbm, factors, out_ref,
    stack, names, name_scalars, row_scalars, ask_packed, blocks, pair_ab, pair_cd, misfit,
    grads, packed, landed, target, gathered,
    name_send, name_recv, block_send, block_recv, send_sem, recv_sem, direct_send, relay_send, all_recv, tile_sem, local_sem,
):
    peers = tiles * rows
    my_tile, my_row = lax.axis_index("tiles"), lax.axis_index("rows")
    me = my_tile * rows + my_row
    slots = stack.shape[0]
    rank = factors.shape[2]
    row_place = lambda peer: my_tile * rows + peer
    far_place = lambda j, k: lax.rem(my_tile + j, tiles) * rows + lax.rem(my_row + k, rows)

    barrier = pltpu.get_barrier_semaphore()
    for j in range(tiles):
        @pl.loop(0 if j else 1, rows, unroll=True)
        def _(k):
            pl.semaphore_signal(barrier, inc=1, device_id=place(far_place(j, k), rows), device_id_type=MESH)

    def tile_copy(slot):
        return pltpu.make_async_copy(tile_hbm.at[slot], stack.at[slot], tile_sem.at[slot])

    names[me] = want_ref[...]
    pl.semaphore_wait(barrier, peers - 1)

    def name_copy(other, slot):
        return pltpu.make_async_remote_copy(
            src_ref=want_ref, dst_ref=names.at[slot], send_sem=name_send.at[other], recv_sem=name_recv.at[slot],
            device_id=place(other, rows), device_id_type=MESH)

    @pl.loop(1, rows, unroll=True)
    def _(k):
        name_copy(row_place(lax.rem(my_row + k, rows)), me).start()

    @pl.loop(1, rows)
    def _(k):
        other = row_place(lax.rem(my_row + k, rows))
        name_copy(other, other).wait_recv()

    bring_names = pltpu.make_async_copy(names.at[pl.ds(my_tile * rows, rows)], row_scalars, local_sem)
    bring_names.start()
    bring_names.wait()

    def block_copy(peer, slot):
        return pltpu.make_async_remote_copy(
            src_ref=ask_packed.at[peer], dst_ref=blocks.at[slot], send_sem=block_send.at[peer], recv_sem=block_recv.at[slot],
            device_id=place(row_place(peer), rows), device_id_type=MESH)

    def read(peer, spot):
        return factors[jnp.maximum(row_scalars[peer, 0, my_row * CAP + spot], 0)].astype(jnp.bfloat16)

    @pl.loop(1, rows, unroll=True)
    def _(k):
        peer = lax.rem(my_row + k, rows)
        for spot in range(CAP):
            ask_packed[peer, spot] = read(peer, spot)
        block_copy(peer, my_row).start()

    for spot in range(CAP):
        blocks[my_row, spot] = read(my_row, spot)

    @pl.loop(1, tiles)
    def _(j):
        @pl.loop(0, rows)
        def _(k):
            name_copy(far_place(j, k), me).start()

    tile_copy(0).start()
    tile_copy(1).start()

    @pl.loop(1, rows)
    def _(k):
        peer = lax.rem(my_row + k, rows)
        block_copy(peer, peer).wait_recv()

    edge = TILE
    chunk = 256
    group = chunk // edge
    def block(slot, mode):
        index = spot_ref[mode, slot]
        return blocks[index // CAP, lax.rem(index, CAP)].astype(jnp.float32)

    def work(slot, before):
        if slot is not None:
            now = slot % 2
            one, two, three, four = (block(slot, mode) for mode in range(4))
            for part in range(edge // group):
                lines = slice(part * group, (part + 1) * group)
                at = pl.ds(part * chunk, chunk)
                pair_ab[now, at, :] = (one[lines][:, None, :] * two[None, :, :]).reshape(chunk, rank).astype(jnp.bfloat16)
                pair_cd[at, :] = (three[lines][:, None, :] * four[None, :, :]).reshape(chunk, rank).astype(jnp.bfloat16)
            tile_copy(slot).wait()
            second = jnp.zeros((edge, rank), jnp.float32)
        if before is not None:
            past = before % 2
            old_three, old_four = block(before, 2), block(before, 3)
            fourth = jnp.zeros((edge, rank), jnp.float32)
        for part in range(edge // group):
            lines = slice(part * group, (part + 1) * group)
            at = pl.ds(part * chunk, chunk)
            if before is not None:
                right = lax.dot_general(misfit[past, :, at], pair_ab[past], (((0,), (0,)), ((), ())), preferred_element_type=jnp.float32)
                right = right.reshape(group, edge, rank)
                grads[before * 4 + 2, lines, :] = jnp.sum(right * old_four[None, :, :], axis=1)
                fourth = fourth + jnp.sum(right * old_three[lines][:, None, :], axis=0)
            if slot is not None:
                model = lax.dot_general(pair_ab[now, at, :], pair_cd[...], (((1,), (1,)), ((), ())), preferred_element_type=jnp.float32)
                off = jnp.clip(model - stack[slot, at, :].astype(jnp.float32), -1.0, 1.0).astype(jnp.bfloat16)
                misfit[now, at, :] = off
                left = jnp.dot(off, pair_cd[...], preferred_element_type=jnp.float32).reshape(group, edge, rank)
                grads[slot * 4, lines, :] = jnp.sum(left * two[None, :, :], axis=1)
                second = second + jnp.sum(left * one[lines][:, None, :], axis=0)
        if slot is not None:
            grads[slot * 4 + 1] = second
        if before is not None:
            grads[before * 4 + 3] = fourth

    work(0, None)

    @pl.loop(1, slots)
    def _(slot):
        @pl.when(slot + 1 < slots)
        def _():
            tile_copy(slot + 1).start()

        work(slot, slot - 1)

    work(None, slots - 1)

    share = TILE // tiles
    span = CAP * share
    total = factors.shape[0] * share

    def message(other, slot):
        return pltpu.make_async_remote_copy(
            src_ref=packed.at[other], dst_ref=landed.at[slot], send_sem=send_sem.at[other], recv_sem=recv_sem.at[slot],
            device_id=place(other, rows), device_id_type=MESH)

    @pl.loop(0, rows)
    def _(k):
        owner = lax.rem(my_row + k, rows)
        found = []
        for spot in range(CAP):
            index = inverse_ref[0, owner * CAP + spot]
            found.append(jnp.where(index >= 0, grads[jnp.maximum(index, 0)], 0.0))
        for tile in range(tiles):
            lines = slice(tile * share, (tile + 1) * share)
            packed[tile * rows + owner] = jnp.concatenate([piece[lines] for piece in found], axis=0).astype(jnp.bfloat16)

        for j in range(1, tiles):
            message(lax.rem(my_tile + j, tiles) * rows + owner, me).start()

        @pl.when(k > 0)
        def _():
            message(row_place(owner), me).start()

    landed[me] = packed[me]

    @pl.loop(1, tiles)
    def _(j):
        @pl.loop(0, rows)
        def _(k):
            other = far_place(j, k)
            name_copy(other, other).wait_recv()

    bring_all = pltpu.make_async_copy(names, name_scalars, local_sem)
    bring_all.start()
    bring_all.wait()
    inside = lax.broadcasted_iota(jnp.int32, (span, LANES), 0)

    @pl.loop(0, peers)
    def _(source):
        base = jnp.zeros((span, LANES), jnp.int32)
        for spot in range(CAP):
            name = name_scalars[source, 0, my_row * CAP + spot]
            line = jnp.where(name >= 0, name * share - spot * share, -(1 << 20))
            base = jnp.where(inside // share == spot, line, base)
        target[pl.ds(source * span, span), :] = base + inside

    marks = [
        jnp.where(target[...] == lax.broadcasted_iota(jnp.int32, (peers * span, LANES), 1) + at, 1.0, 0.0).astype(jnp.bfloat16)
        for at in range(0, total, LANES)
    ]

    @pl.loop(1, peers)
    def _(k):
        other = lax.rem(me + k, peers)
        message(other, other).wait_recv()

    everything = landed[...].reshape(peers * span, rank)
    for at, mark in zip(range(0, total, LANES), marks):
        size = min(LANES, total - at)
        summed = lax.dot_general(mark, everything, (((0,), (0,)), ((), ())), preferred_element_type=jnp.float32)
        gathered[my_tile, pl.ds(at, size), :] = summed[:size].astype(jnp.bfloat16)

    def spread(towards, share_at, sems):
        return pltpu.make_async_remote_copy(
            src_ref=gathered.at[share_at], dst_ref=gathered.at[share_at], send_sem=sems, recv_sem=all_recv.at[share_at],
            device_id=place(towards * rows + my_row, rows), device_id_type=MESH)

    last = tiles - 1

    def each_direct(act):
        for away in range(last - 1, 0, -1):
            @pl.when(my_tile + away < tiles)
            def _():
                act(spread(my_tile + away, my_tile, direct_send.at[my_tile + away]))

            @pl.when(my_tile >= away)
            def _():
                act(spread(my_tile - away, my_tile, direct_send.at[my_tile - away]))

    def each_relay(tile, act):
        @pl.when((tile == 0) & (my_tile == last - 1))
        def _():
            act(spread(last, 0, relay_send.at[0]))

        @pl.when((tile == last) & (my_tile == 1))
        def _():
            act(spread(0, last, relay_send.at[1]))

    per = 16 // share

    def update(tile):
        if share % 8:
            return
        lines = pl.ds(pl.multiple_of(tile * share, share), share)

        @pl.loop(0, total // 16, unroll=4)
        def _(i):
            values = gathered[tile, pl.ds(pl.multiple_of(i * 16, 16), 16), :].astype(jnp.float32)
            for piece in range(per):
                name = i * per + piece
                out_ref[name, lines, :] = factors[name, lines, :] - step_size * values[piece * share:(piece + 1) * share]

    each_direct(lambda copy: copy.start())
    update(my_tile)

    for away in (2, 1) + tuple(range(3, tiles)):
        both = ((my_tile - away, my_tile >= away), (my_tile + away, my_tile + away < tiles))
        for tile, inside_chain in both:
            @pl.when(inside_chain)
            def _():
                spread(my_tile, tile, direct_send.at[my_tile]).wait_recv()
                each_relay(tile, lambda copy: copy.start())

        for tile, inside_chain in both:
            @pl.when(inside_chain)
            def _():
                update(tile)

    if share % 8:
        for at in range(0, total, 16):
            values = [gathered[tile, pl.ds(at, 16), :].astype(jnp.float32) for tile in range(tiles)]
            for piece in range(per):
                name = at // share + piece
                whole = jnp.concatenate([value[piece * share:(piece + 1) * share] for value in values], axis=0)
                out_ref[name] = factors[name] - step_size * whole

    each_direct(lambda copy: copy.wait_send())
    each_relay(0, lambda copy: copy.wait_send())
    each_relay(last, lambda copy: copy.wait_send())

    @pl.loop(1, rows)
    def _(k):
        peer = lax.rem(my_row + k, rows)
        block_copy(peer, my_row).wait_send()

    @pl.loop(1, peers)
    def _(k):
        other = lax.rem(me + k, peers)
        name_copy(other, me).wait_send()
        message(other, me).wait_send()


def step(spot, inverse, want, tile_stack, factors, tiles, rows):
    peers = tiles * rows
    slots, height, width = tile_stack.shape
    local, edge, rank = factors.shape
    share = TILE // tiles
    span = CAP * share
    dma = lambda *shape: pltpu.SemaphoreType.DMA(shape)
    bf16 = lambda *shape: pltpu.VMEM(shape, jnp.bfloat16)
    return pl.pallas_call(
        functools.partial(step_kernel, tiles, rows),
        out_shape=jax.ShapeDtypeStruct((local, edge, rank), jnp.float32),
        in_specs=[pl.BlockSpec(memory_space=pltpu.SMEM)] * 2 + [pl.BlockSpec(memory_space=pltpu.VMEM), pl.BlockSpec(memory_space=pl.ANY), pl.BlockSpec(memory_space=pltpu.VMEM)],
        out_specs=pl.BlockSpec(memory_space=pltpu.VMEM),
        scratch_shapes=[
            bf16(slots, height, width),
            pltpu.VMEM((peers, 1, LANES), jnp.int32),
            pltpu.SMEM((peers, 1, LANES), jnp.int32),
            pltpu.SMEM((rows, 1, LANES), jnp.int32),
            bf16(rows, CAP, TILE, rank),
            bf16(rows, CAP, TILE, rank),
            bf16(2, height, rank), bf16(width, rank), bf16(2, height, width),
            pltpu.VMEM((slots * 4, TILE, rank), jnp.float32),
            bf16(peers, span, rank),
            bf16(peers, span, rank),
            pltpu.VMEM((peers * span, LANES), jnp.int32),
            bf16(tiles, local * share, rank),
            dma(peers), dma(peers), dma(rows), dma(rows), dma(peers), dma(peers),
            dma(tiles), dma(2), dma(tiles), dma(slots), pltpu.SemaphoreType.DMA,
        ],
        compiler_params=pltpu.CompilerParams(collective_id=0, has_side_effects=True, vmem_limit_bytes=40 << 20),
        cost_estimate=pl.CostEstimate(flops=6 * slots * height * width * rank, bytes_accessed=2 * slots * height * width, transcendentals=0),
        name="gradient_step",
    )(spot, inverse, want, tile_stack, factors)


def tables(coords, live_count, local_blocks):
    flat = coords.T
    owner = flat // local_blocks
    mode = lax.broadcasted_iota(jnp.int32, flat.shape, 0)
    slot = lax.broadcasted_iota(jnp.int32, flat.shape, 1)
    order = slot * 4 + mode
    live = slot < live_count
    earlier = (owner == owner[:, :, None, None]) & live & (order < order[:, :, None, None])
    spot = owner * CAP + jnp.sum(earlier.astype(jnp.int32), axis=(2, 3))
    spot = jnp.where(live, spot, -1)
    hit = spot == jnp.arange(LANES)[:, None, None]
    block = mode * local_blocks + flat - owner * local_blocks
    want = jnp.max(jnp.where(hit, block, -1), axis=(1, 2))
    inverse = jnp.max(jnp.where(hit, order, -1), axis=(1, 2))
    return jnp.maximum(spot, 0), want.reshape(1, LANES), inverse.reshape(1, LANES)


def on_device(tile_values, tile_coords, tile_count, factors):
    tiles, rows = lax.axis_size("tiles"), lax.axis_size("rows")
    modes, local_rows, rank = factors.shape
    spot, want, inverse = tables(tile_coords[0], tile_count[0], local_rows // TILE)
    updated = step(spot, inverse, want, tile_values[0], factors.reshape(-1, TILE, rank), tiles, rows)
    return updated.reshape(factors.shape)


def solution(mesh):
    return jax.shard_map(
        on_device,
        mesh=mesh,
        in_specs=(
            P(("tiles", "rows"), None, None, None),
            P(("tiles", "rows"), None, None),
            P(("tiles", "rows")),
            P(None, "rows", None),
        ),
        out_specs=P(None, "rows", None),
        check_vma=False,
    )
```

```python
import functools

import jax
import jax.numpy as jnp
from jax import lax
from jax.experimental import pallas as pl
from jax.experimental.pallas import tpu as pltpu
from jax.sharding import PartitionSpec as P

TILE = 32
CAP = 4
LANES = 128
MESH = pl.DeviceIdType.MESH

step_size = 0.02


def place(index, rows):
    return {"tiles": index // rows, "rows": lax.rem(index, rows)}


def step_kernel(
    tiles, rows, spot_ref, inverse_ref, want_ref, tile_hbm, factors, out_ref,
    stack, names, name_scalars, row_scalars, ask_packed, blocks, pair_ab, pair_cd, misfit,
    grads, packed, landed, target, gathered,
    name_send, name_recv, block_send, block_recv, send_sem, recv_sem, direct_send, relay_send, all_recv, tile_sem, local_sem,
):
    peers = tiles * rows
    my_tile, my_row = lax.axis_index("tiles"), lax.axis_index("rows")
    me = my_tile * rows + my_row
    slots = stack.shape[0]
    rank = factors.shape[2]
    row_place = lambda peer: my_tile * rows + peer
    far_place = lambda j, k: lax.rem(my_tile + j, tiles) * rows + lax.rem(my_row + k, rows)

    barrier = pltpu.get_barrier_semaphore()
    for j in range(tiles):
        @pl.loop(0 if j else 1, rows, unroll=True)
        def _(k):
            pl.semaphore_signal(barrier, inc=1, device_id=place(far_place(j, k), rows), device_id_type=MESH)

    def tile_copy(slot):
        return pltpu.make_async_copy(tile_hbm.at[slot], stack.at[slot], tile_sem.at[slot])

    names[me] = want_ref[...]
    pl.semaphore_wait(barrier, peers - 1)

    def name_copy(other, slot):
        return pltpu.make_async_remote_copy(
            src_ref=want_ref, dst_ref=names.at[slot], send_sem=name_send.at[other], recv_sem=name_recv.at[slot],
            device_id=place(other, rows), device_id_type=MESH)

    @pl.loop(1, rows, unroll=True)
    def _(k):
        name_copy(row_place(lax.rem(my_row + k, rows)), me).start()

    @pl.loop(1, rows)
    def _(k):
        other = row_place(lax.rem(my_row + k, rows))
        name_copy(other, other).wait_recv()

    bring_names = pltpu.make_async_copy(names.at[pl.ds(my_tile * rows, rows)], row_scalars, local_sem)
    bring_names.start()
    bring_names.wait()

    def block_copy(peer, slot):
        return pltpu.make_async_remote_copy(
            src_ref=ask_packed.at[peer], dst_ref=blocks.at[slot], send_sem=block_send.at[peer], recv_sem=block_recv.at[slot],
            device_id=place(row_place(peer), rows), device_id_type=MESH)

    def read(peer, spot):
        return factors[jnp.maximum(row_scalars[peer, 0, my_row * CAP + spot], 0)].astype(jnp.bfloat16)

    @pl.loop(1, rows, unroll=True)
    def _(k):
        peer = lax.rem(my_row + k, rows)
        for spot in range(CAP):
            ask_packed[peer, spot] = read(peer, spot)
        block_copy(peer, my_row).start()

    for spot in range(CAP):
        blocks[my_row, spot] = read(my_row, spot)

    @pl.loop(1, tiles)
    def _(j):
        @pl.loop(0, rows)
        def _(k):
            name_copy(far_place(j, k), me).start()

    tile_copy(0).start()
    tile_copy(1).start()

    @pl.loop(1, rows)
    def _(k):
        peer = lax.rem(my_row + k, rows)
        block_copy(peer, peer).wait_recv()

    edge = TILE
    chunk = 512
    group = chunk // edge
    def block(slot, mode):
        index = spot_ref[mode, slot]
        return blocks[index // CAP, lax.rem(index, CAP)].astype(jnp.float32)

    @pl.loop(0, slots)
    def _(slot):
        @pl.when(slot + 2 < slots)
        def _():
            tile_copy(slot + 2).start()

        one, two, three, four = (block(slot, mode) for mode in range(4))
        for part in range(edge // group):
            lines = slice(part * group, (part + 1) * group)
            at = pl.ds(part * chunk, chunk)
            pair_ab[at, :] = (one[lines][:, None, :] * two[None, :, :]).reshape(chunk, rank).astype(jnp.bfloat16)
            pair_cd[at, :] = (three[lines][:, None, :] * four[None, :, :]).reshape(chunk, rank).astype(jnp.bfloat16)
        tile_copy(slot).wait()
        second = jnp.zeros((edge, rank), jnp.float32)
        for part in range(edge // group):
            lines = slice(part * group, (part + 1) * group)
            at = pl.ds(part * chunk, chunk)
            model = lax.dot_general(pair_ab[at, :], pair_cd[...], (((1,), (1,)), ((), ())), preferred_element_type=jnp.float32)
            off = jnp.clip(model - stack[slot, at, :].astype(jnp.float32), -1.0, 1.0).astype(jnp.bfloat16)
            misfit[at, :] = off
            left = jnp.dot(off, pair_cd[...], preferred_element_type=jnp.float32).reshape(group, edge, rank)
            grads[slot * 4, lines, :] = jnp.sum(left * two[None, :, :], axis=1)
            second = second + jnp.sum(left * one[lines][:, None, :], axis=0)
        grads[slot * 4 + 1] = second
        fourth = jnp.zeros((edge, rank), jnp.float32)
        for part in range(edge // group):
            lines = slice(part * group, (part + 1) * group)
            at = pl.ds(part * chunk, chunk)
            right = lax.dot_general(misfit[:, at], pair_ab[...], (((0,), (0,)), ((), ())), preferred_element_type=jnp.float32)
            right = right.reshape(group, edge, rank)
            grads[slot * 4 + 2, lines, :] = jnp.sum(right * four[None, :, :], axis=1)
            fourth = fourth + jnp.sum(right * three[lines][:, None, :], axis=0)
        grads[slot * 4 + 3] = fourth

    share = TILE // tiles
    span = CAP * share
    total = factors.shape[0] * share

    def message(other, slot):
        return pltpu.make_async_remote_copy(
            src_ref=packed.at[other], dst_ref=landed.at[slot], send_sem=send_sem.at[other], recv_sem=recv_sem.at[slot],
            device_id=place(other, rows), device_id_type=MESH)

    @pl.loop(0, rows)
    def _(k):
        owner = lax.rem(my_row + k, rows)
        found = []
        for spot in range(CAP):
            index = inverse_ref[0, owner * CAP + spot]
            found.append(jnp.where(index >= 0, grads[jnp.maximum(index, 0)], 0.0))
        for tile in range(tiles):
            lines = slice(tile * share, (tile + 1) * share)
            packed[tile * rows + owner] = jnp.concatenate([piece[lines] for piece in found], axis=0).astype(jnp.bfloat16)

        for j in range(1, tiles):
            message(lax.rem(my_tile + j, tiles) * rows + owner, me).start()

        @pl.when(k > 0)
        def _():
            message(row_place(owner), me).start()

    landed[me] = packed[me]

    @pl.loop(1, tiles)
    def _(j):
        @pl.loop(0, rows)
        def _(k):
            other = far_place(j, k)
            name_copy(other, other).wait_recv()

    bring_all = pltpu.make_async_copy(names, name_scalars, local_sem)
    bring_all.start()
    bring_all.wait()
    inside = lax.broadcasted_iota(jnp.int32, (span, LANES), 0)

    @pl.loop(0, peers)
    def _(source):
        base = jnp.zeros((span, LANES), jnp.int32)
        for spot in range(CAP):
            name = name_scalars[source, 0, my_row * CAP + spot]
            line = jnp.where(name >= 0, name * share - spot * share, -(1 << 20))
            base = jnp.where(inside // share == spot, line, base)
        target[pl.ds(source * span, span), :] = base + inside

    marks = [
        jnp.where(target[...] == lax.broadcasted_iota(jnp.int32, (peers * span, LANES), 1) + at, 1.0, 0.0).astype(jnp.bfloat16)
        for at in range(0, total, LANES)
    ]

    @pl.loop(1, peers)
    def _(k):
        other = lax.rem(me + k, peers)
        message(other, other).wait_recv()

    everything = landed[...].reshape(peers * span, rank)
    for at, mark in zip(range(0, total, LANES), marks):
        size = min(LANES, total - at)
        summed = lax.dot_general(mark, everything, (((0,), (0,)), ((), ())), preferred_element_type=jnp.float32)
        gathered[my_tile, pl.ds(at, size), :] = summed[:size].astype(jnp.bfloat16)

    def spread(towards, share_at, sems):
        return pltpu.make_async_remote_copy(
            src_ref=gathered.at[share_at], dst_ref=gathered.at[share_at], send_sem=sems, recv_sem=all_recv.at[share_at],
            device_id=place(towards * rows + my_row, rows), device_id_type=MESH)

    last = tiles - 1

    def each_direct(act):
        for away in range(last - 1, 0, -1):
            @pl.when(my_tile + away < tiles)
            def _():
                act(spread(my_tile + away, my_tile, direct_send.at[my_tile + away]))

            @pl.when(my_tile >= away)
            def _():
                act(spread(my_tile - away, my_tile, direct_send.at[my_tile - away]))

    def each_relay(tile, act):
        @pl.when((tile == 0) & (my_tile == last - 1))
        def _():
            act(spread(last, 0, relay_send.at[0]))

        @pl.when((tile == last) & (my_tile == 1))
        def _():
            act(spread(0, last, relay_send.at[1]))

    per = 16 // share

    def update(tile):
        if share % 8:
            return
        lines = pl.ds(pl.multiple_of(tile * share, share), share)

        @pl.loop(0, total // 16, unroll=4)
        def _(i):
            values = gathered[tile, pl.ds(pl.multiple_of(i * 16, 16), 16), :].astype(jnp.float32)
            for piece in range(per):
                name = i * per + piece
                out_ref[name, lines, :] = factors[name, lines, :] - step_size * values[piece * share:(piece + 1) * share]

    each_direct(lambda copy: copy.start())
    update(my_tile)

    for away in (2, 1) + tuple(range(3, tiles)):
        both = ((my_tile - away, my_tile >= away), (my_tile + away, my_tile + away < tiles))
        for tile, inside_chain in both:
            @pl.when(inside_chain)
            def _():
                spread(my_tile, tile, direct_send.at[my_tile]).wait_recv()
                each_relay(tile, lambda copy: copy.start())

        for tile, inside_chain in both:
            @pl.when(inside_chain)
            def _():
                update(tile)

    if share % 8:
        for at in range(0, total, 16):
            values = [gathered[tile, pl.ds(at, 16), :].astype(jnp.float32) for tile in range(tiles)]
            for piece in range(per):
                name = at // share + piece
                whole = jnp.concatenate([value[piece * share:(piece + 1) * share] for value in values], axis=0)
                out_ref[name] = factors[name] - step_size * whole

    each_direct(lambda copy: copy.wait_send())
    each_relay(0, lambda copy: copy.wait_send())
    each_relay(last, lambda copy: copy.wait_send())

    @pl.loop(1, rows)
    def _(k):
        peer = lax.rem(my_row + k, rows)
        block_copy(peer, my_row).wait_send()

    @pl.loop(1, peers)
    def _(k):
        other = lax.rem(me + k, peers)
        name_copy(other, me).wait_send()
        message(other, me).wait_send()


def step(spot, inverse, want, tile_stack, factors, tiles, rows):
    peers = tiles * rows
    slots, height, width = tile_stack.shape
    local, edge, rank = factors.shape
    share = TILE // tiles
    span = CAP * share
    dma = lambda *shape: pltpu.SemaphoreType.DMA(shape)
    bf16 = lambda *shape: pltpu.VMEM(shape, jnp.bfloat16)
    return pl.pallas_call(
        functools.partial(step_kernel, tiles, rows),
        out_shape=jax.ShapeDtypeStruct((local, edge, rank), jnp.float32),
        in_specs=[pl.BlockSpec(memory_space=pltpu.SMEM)] * 2 + [pl.BlockSpec(memory_space=pltpu.VMEM), pl.BlockSpec(memory_space=pl.ANY), pl.BlockSpec(memory_space=pltpu.VMEM)],
        out_specs=pl.BlockSpec(memory_space=pltpu.VMEM),
        scratch_shapes=[
            bf16(slots, height, width),
            pltpu.VMEM((peers, 1, LANES), jnp.int32),
            pltpu.SMEM((peers, 1, LANES), jnp.int32),
            pltpu.SMEM((rows, 1, LANES), jnp.int32),
            bf16(rows, CAP, TILE, rank),
            bf16(rows, CAP, TILE, rank),
            bf16(height, rank), bf16(width, rank), bf16(height, width),
            pltpu.VMEM((slots * 4, TILE, rank), jnp.float32),
            bf16(peers, span, rank),
            bf16(peers, span, rank),
            pltpu.VMEM((peers * span, LANES), jnp.int32),
            bf16(tiles, local * share, rank),
            dma(peers), dma(peers), dma(rows), dma(rows), dma(peers), dma(peers),
            dma(tiles), dma(2), dma(tiles), dma(slots), pltpu.SemaphoreType.DMA,
        ],
        compiler_params=pltpu.CompilerParams(collective_id=0, has_side_effects=True, vmem_limit_bytes=40 << 20),
        cost_estimate=pl.CostEstimate(flops=6 * slots * height * width * rank, bytes_accessed=2 * slots * height * width, transcendentals=0),
        name="gradient_step",
    )(spot, inverse, want, tile_stack, factors)


def tables(coords, live_count, local_blocks):
    flat = coords.T
    owner = flat // local_blocks
    mode = lax.broadcasted_iota(jnp.int32, flat.shape, 0)
    slot = lax.broadcasted_iota(jnp.int32, flat.shape, 1)
    order = slot * 4 + mode
    live = slot < live_count
    earlier = (owner == owner[:, :, None, None]) & live & (order < order[:, :, None, None])
    spot = owner * CAP + jnp.sum(earlier.astype(jnp.int32), axis=(2, 3))
    spot = jnp.where(live, spot, -1)
    hit = spot == jnp.arange(LANES)[:, None, None]
    block = mode * local_blocks + flat - owner * local_blocks
    want = jnp.max(jnp.where(hit, block, -1), axis=(1, 2))
    inverse = jnp.max(jnp.where(hit, order, -1), axis=(1, 2))
    return jnp.maximum(spot, 0), want.reshape(1, LANES), inverse.reshape(1, LANES)


def on_device(tile_values, tile_coords, tile_count, factors):
    tiles, rows = lax.axis_size("tiles"), lax.axis_size("rows")
    modes, local_rows, rank = factors.shape
    spot, want, inverse = tables(tile_coords[0], tile_count[0], local_rows // TILE)
    updated = step(spot, inverse, want, tile_values[0], factors.reshape(-1, TILE, rank), tiles, rows)
    return updated.reshape(factors.shape)


def solution(mesh):
    return jax.shard_map(
        on_device,
        mesh=mesh,
        in_specs=(
            P(("tiles", "rows"), None, None, None),
            P(("tiles", "rows"), None, None),
            P(("tiles", "rows")),
            P(None, "rows", None),
        ),
        out_specs=P(None, "rows", None),
        check_vma=False,
    )
```
